256 devices in a mesh: dp: 256 (over z, y, x, core).
Axes of the slice: x: 4, y: 4, z: 8, core: 2. Of those that a mesh axis runs over, the one named last changes fastest.
Arguments:
- image_emb: bfloat16 [262144, 1152], P('dp'), may hold values from -0.1875 to 0.1875
- text_emb: bfloat16 [262144, 1152], P('dp'), may hold values from -0.1875 to 0.1875
- cosine_multiplier: float32 [1], replicated, may hold values from 5 to 20
- logit_bias: float32 [1], replicated, may hold values from -5 to -2
Outputs:
- image_grad: bfloat16 [262144, 1152], P('dp')
- text_grad: bfloat16 [262144, 1152], P('dp')
The draws below stay inside these ranges and needn't reach their ends.
All inputs are finite; a program needn't handle non-finite values.
Results may differ from the reference program's by a relative error of at most 0.0063.
Values may be sent and summed in bfloat16 or wider, within the bound.
No kernel may reach another device: no remote copies, remote signals or barrier semaphores. Data moves between devices by JAX's collectives and lax.ppermute only.
A program may use at most 64 MiB of HBM per device.

```python
import math
import jax
import jax.numpy as jnp
from jax import lax

D = 1152
ROWS = 1024
SHIFTS = 2
BATCH = 262144
N_DP = 256


def shard_levels(rng, extent, cuts, low, top_value):
    def one(position, blocks):
        draws = jax.random.uniform(jax.random.fold_in(jax.random.fold_in(rng, 6), position), (blocks,), jnp.float32, low / len(cuts), top_value / len(cuts))
        return jnp.repeat(jnp.exp(draws), extent[position] // blocks).reshape((-1,) + (1,) * (len(extent) - position - 1))

    gain = one(*cuts[0])
    for cut in cuts[1:]:
        gain = gain * one(*cut)
    return gain


def gaussian(own_key, shape, spread, reach, shards=(), kind=jnp.bfloat16):
    level = shard_levels(own_key, shape, shards, -0.22, 0.18) if shards else 1.0
    values = jax.random.normal(own_key, shape, jnp.float32) * spread * level
    return jnp.minimum(jnp.maximum(values, -reach), reach).astype(kind)


def setup_inputs(seed: int = 0) -> dict:
    splits = jax.random.split(jax.random.key(seed), 5)
    return {
        "image_emb": gaussian(splits[0], (BATCH, D), (D ** -0.5), 0.1875, ((0, 256),)),
        "text_emb": gaussian(splits[1], (BATCH, D), (D ** -0.5), 0.1875, ((0, 256),)),
        "cosine_multiplier": jnp.clip(jnp.exp(jax.random.uniform(splits[2], (1,), jnp.float32, math.log(5.0), math.log(20.0))), 5.0, 20.0),
        "logit_bias": jnp.clip(jax.random.uniform(splits[3], (1,), jnp.float32, -5.0, -2.0), -5.0, -2.0),
    }


epsilon = 1e-06

def normalize(values):
    floats = values.astype(jnp.float32)
    inverse = lax.rsqrt(lax.optimization_barrier(jnp.sum(floats * floats, axis=-1, keepdims=True)) + epsilon)
    return (floats * inverse, inverse)

def norm_backward(normed, inverse, upstream):
    inner = lax.optimization_barrier(jnp.sum(normed * upstream, axis=-1, keepdims=True))
    return (inverse * (upstream - normed * inner)).astype(jnp.bfloat16)

def objective_factors(picture_count, caption_count, steepness_factor, moved_intercept, matching_indicator):
    couple_scores = steepness_factor * jnp.dot(picture_count, caption_count.T, preferred_element_type=jnp.float32) + moved_intercept
    if matching_indicator:
        desired_signs = 2.0 * jnp.eye(picture_count.shape[0], dtype=jnp.float32) - 1.0
        couple_factors = -desired_signs * jax.nn.sigmoid(-desired_signs * couple_scores) * steepness_factor
    else:
        couple_factors = jax.nn.sigmoid(couple_scores) * steepness_factor
    return couple_factors.astype(jnp.bfloat16)

def reference(image_emb, text_emb, cosine_multiplier, logit_bias):
    steepness_factor = cosine_multiplier[0]
    moved_intercept = logit_bias[0]
    y_img, inv_img = normalize(image_emb)
    y_txt, inv_txt = normalize(text_emb)
    picture_features = y_img.astype(jnp.bfloat16).reshape(N_DP, ROWS, D)
    caption_features = y_txt.astype(jnp.bfloat16).reshape(N_DP, ROWS, D)

    def image_block(couple_segment):
        total = jnp.zeros((ROWS, D), jnp.float32)
        for segment_start in range(SHIFTS):
            neighbour_processor = caption_features[(couple_segment - segment_start) % N_DP]
            couple_factors = objective_factors(picture_features[couple_segment], neighbour_processor, steepness_factor, moved_intercept, segment_start == 0)
            total = total + jnp.dot(couple_factors, neighbour_processor, preferred_element_type=jnp.float32)
        return total

    def text_block(couple_segment):
        total = jnp.zeros((ROWS, D), jnp.float32)
        for segment_start in range(SHIFTS):
            incoming_entries = picture_features[(couple_segment + segment_start) % N_DP]
            couple_factors = objective_factors(incoming_entries, caption_features[couple_segment], steepness_factor, moved_intercept, segment_start == 0)
            term = jnp.dot(couple_factors.T, incoming_entries, preferred_element_type=jnp.float32)
            if segment_start > 0:
                term = lax.optimization_barrier(term.astype(jnp.bfloat16)).astype(jnp.float32)
            total = total + term
        return total
    blocks = jnp.arange(N_DP, dtype=jnp.int32)
    grad_zimg = lax.map(image_block, blocks).reshape(BATCH, D)
    grad_ztxt = lax.map(text_block, blocks).reshape(BATCH, D)
    return (norm_backward(y_img, inv_img, grad_zimg), norm_backward(y_txt, inv_txt, grad_ztxt))
```

```python
import functools

import jax
import jax.numpy as jnp
from jax import lax
from jax.experimental import pallas as pl
from jax.experimental.pallas import tpu as pltpu
from jax.sharding import PartitionSpec as P

epsilon = 1e-06
LOG2_E = 1.4426950408889634
F32, BF16 = jnp.float32, jnp.bfloat16
BLOCK = 256
FIRST = 768
MIB = 2**20

VMEM = pl.BlockSpec(memory_space=pltpu.VMEM)
SMEM = pl.BlockSpec(memory_space=pltpu.SMEM)
HBM = pl.BlockSpec(memory_space=pl.ANY)


def rows_dot_rows(a, b):
    return lax.dot_general(a, b, (((1,), (1,)), ((), ())), preferred_element_type=F32)


def columns_dot(a, b):
    return lax.dot_general(a, b, (((0,), (0,)), ((), ())), preferred_element_type=F32)


def dot(a, b):
    return jnp.dot(a, b, preferred_element_type=F32)


def blocks(rows):
    return [slice(start, start + BLOCK) for start in range(0, rows, BLOCK)]


def fetch(parity, if_even, if_odd, start, target, sems):
    for i, here in enumerate(blocks(target.shape[0])):
        there = pl.ds(start + here.start, BLOCK)

        @pl.when(parity == 0)
        def _():
            pltpu.make_async_copy(if_even.at[there], target.at[here], sems.at[i]).start()

        @pl.when(parity == 1)
        def _():
            pltpu.make_async_copy(if_odd.at[there], target.at[here], sems.at[i]).start()


def arrived(source, target, sems, i, here):
    pltpu.make_async_copy(source.at[pl.ds(0, BLOCK)], target.at[here], sems.at[i]).wait()


def normalize_block(raw):
    floats = raw.astype(F32)
    inverse = lax.rsqrt(jnp.sum(floats * floats, axis=-1, keepdims=True) + epsilon)
    return (floats * inverse).astype(BF16), inverse


def first_kernel(parity_ref, image, text, z1, raw1, inv1, sems):
    fetch(parity_ref[0], image, text, 0, raw1, sems)
    for i, here in enumerate(blocks(raw1.shape[0])):
        arrived(image, raw1, sems, i, here)
        z1[here, :], inv1[here, :] = normalize_block(raw1[here, :])


def rest_kernel(
    parity_ref, image, text, z1, zp, z2, zq, rawp, raw2, invp, inv2, semsp, sems2
):
    first = z1.shape[0]
    fetch(parity_ref[0], text, image, 0, rawp, semsp)
    fetch(parity_ref[0], image, text, first, raw2, sems2)
    for i, here in enumerate(blocks(rawp.shape[0])):
        arrived(image, rawp, semsp, i, here)
        zp[here, :], invp[here, :] = normalize_block(rawp[here, :])
    zq[:first, :] = z1[...]
    for i, here in enumerate(blocks(raw2.shape[0])):
        arrived(image, raw2, sems2, i, here)
        normed, inv2[here, :] = normalize_block(raw2[here, :])
        z2[here, :] = normed
        zq[pl.ds(first + here.start, BLOCK), :] = normed


def exponential(agreement, scale, shift):
    return jnp.exp2(agreement * scale + shift)


def local_kernel(multiplier_ref, bias_ref, zp, zq, coef, gq):
    multiplier = multiplier_ref[0]
    scale, shift = -multiplier * LOG2_E, -bias_ref[0] * LOG2_E
    count = zq.shape[0]
    for here in blocks(zp.shape[0]):
        power = exponential(rows_dot_rows(zp[here, :], zq[...]), scale, shift)
        value = multiplier / (1.0 + power)
        row = lax.broadcasted_iota(jnp.int32, (BLOCK, count), 0) + here.start
        column = lax.broadcasted_iota(jnp.int32, (BLOCK, count), 1)
        coef[here, :] = jnp.where(row == column, -power * value, value).astype(BF16)
    for here in blocks(count):
        gq[here, :] = columns_dot(coef[:, here], zp[...])


def remote_coef(own, other, multiplier, scale, shift):
    power = exponential(rows_dot_rows(own, other), scale, shift)
    return (multiplier / (1.0 + power)).astype(BF16)


def backward_block(raw, inverse, upstream):
    floats = raw.astype(F32)
    inner = jnp.sum(floats * upstream, axis=-1, keepdims=True)
    return (inverse * (upstream - floats * (inverse * inverse * inner))).astype(BF16)


def put(parity, if_even, if_odd, there, source, sem):
    @pl.when(parity == 0)
    def _():
        pltpu.make_async_copy(source, if_even.at[there], sem).start()

    @pl.when(parity == 1)
    def _():
        pltpu.make_async_copy(source, if_odd.at[there], sem).start()


def near_kernel(
    parity_ref, multiplier_ref, bias_ref, zp, zq, coef, other, rawp, invp, image_out, text_out, token, held, sems
):
    token[...] = jnp.zeros_like(token)
    multiplier = multiplier_ref[0]
    scale, shift = -multiplier * LOG2_E, -bias_ref[0] * LOG2_E
    for i, here in enumerate(blocks(zp.shape[0])):
        factors = remote_coef(zp[here, :], other[...], multiplier, scale, shift)
        total = dot(coef[here, :], zq[...]) + dot(factors, other[...])
        held[here, :] = backward_block(rawp[here, :], invp[here, :], total)
        put(parity_ref[0], text_out, image_out, here, held.at[here], sems.at[i])
    for i, here in enumerate(blocks(zp.shape[0])):
        pltpu.make_async_copy(held.at[here], image_out.at[here], sems.at[i]).wait()


def far_kernel(multiplier_ref, bias_ref, zq, other, gq, after_near, total):
    multiplier = multiplier_ref[0]
    scale, shift = -multiplier * LOG2_E, -bias_ref[0] * LOG2_E
    for here in blocks(zq.shape[0]):
        factors = remote_coef(zq[here, :], other[...], multiplier, scale, shift)
        total[here, :] = gq[here, :] + dot(factors, other[...])


def last_kernel(
    parity_ref, multiplier_ref, bias_ref, zq, other, gq, raw1, raw2, inv1, inv2, image_in, text_in, image_out, text_out, held, sems
):
    multiplier = multiplier_ref[0]
    scale, shift = -multiplier * LOG2_E, -bias_ref[0] * LOG2_E
    first = raw1.shape[0]
    for i, here in enumerate(blocks(zq.shape[0])):
        factors = remote_coef(zq[here, :], other[...], multiplier, scale, shift)
        total = gq[here, :] + dot(factors, other[...])
        if here.start < first:
            raw, inverse = raw1[here, :], inv1[here, :]
        else:
            there = slice(here.start - first, here.stop - first)
            raw, inverse = raw2[there, :], inv2[there, :]
        held[here, :] = backward_block(raw, inverse, total)
        put(parity_ref[0], image_out, text_out, here, held.at[here], sems.at[i])
    for i, here in enumerate(blocks(zq.shape[0])):
        pltpu.make_async_copy(held.at[here], image_out.at[here], sems.at[i]).wait()


def shape(rows, columns, kind):
    return jax.ShapeDtypeStruct((rows, columns), kind)


def call(kernel, out_shape, in_specs, out_specs, scratch, limit, flops, **more):
    return pl.pallas_call(
        kernel,
        out_shape=out_shape,
        in_specs=in_specs,
        out_specs=out_specs,
        scratch_shapes=scratch,
        compiler_params=pltpu.CompilerParams(vmem_limit_bytes=limit * MIB),
        cost_estimate=pl.CostEstimate(flops=flops // 64, bytes_accessed=1024, transcendentals=0),
        **more,
    )


def on_device(image_emb, text_emb, cosine_multiplier, logit_bias):
    rows, width = image_emb.shape
    count = lax.axis_size("dp")
    parity = (lax.axis_index("dp") % 2).astype(jnp.int32).reshape(1)
    near = [(e, e ^ 1) for e in range(count)]
    far = [(e, (e - 1) % count if e % 2 == 0 else (e + 1) % count) for e in range(count)]
    first, rest = FIRST, rows - FIRST
    image_emb = pltpu.with_memory_space_constraint(image_emb, pltpu.HBM)
    text_emb = pltpu.with_memory_space_constraint(text_emb, pltpu.HBM)
    dma = pltpu.SemaphoreType.DMA
    product = 2 * rows * rows * width

    z1, raw1, inv1 = call(
        first_kernel,
        (shape(first, width, BF16), shape(first, width, BF16), shape(first, 1, F32)),
        [SMEM, HBM, HBM], (VMEM,) * 3, [dma((first // BLOCK,))], 4, product // 8,
    )(parity, image_emb, text_emb)
    far1 = lax.ppermute(z1, "dp", far)
    zp, z2, zq, rawp, raw2, invp, inv2 = call(
        rest_kernel,
        (
            shape(rows, width, BF16), shape(rest, width, BF16), shape(rows, width, BF16),
            shape(rows, width, BF16), shape(rest, width, BF16), shape(rows, 1, F32), shape(rest, 1, F32),
        ),
        [SMEM, HBM, HBM, VMEM], (VMEM,) * 7, [dma((rows // BLOCK,)), dma((rest // BLOCK,))], 4, product // 4,
    )(parity, image_emb, text_emb, z1)
    near_block = lax.ppermute(zp, "dp", near)
    far2 = lax.ppermute(z2, "dp", far)
    coef, gq = call(
        local_kernel,
        (shape(rows, rows, BF16), shape(rows, width, F32)),
        [SMEM, SMEM, VMEM, VMEM], (VMEM,) * 2, [], 8, 2 * product,
    )(cosine_multiplier, logit_bias, zp, zq)
    image_out, text_out, token = call(
        near_kernel,
        (pltpu.HBM((rows, width), BF16),) * 2 + (shape(8, 128, F32),),
        [SMEM] * 3 + [VMEM] * 6, (HBM, HBM, VMEM),
        [pltpu.VMEM((rows, width), BF16), dma((rows // BLOCK,))], 12, 3 * product,
    )(parity, cosine_multiplier, logit_bias, zp, zq, coef, near_block, rawp, invp)
    gq = call(
        far_kernel, shape(rows, width, F32),
        [SMEM, SMEM, VMEM, VMEM, VMEM, VMEM], VMEM, [], 8, 2 * product * first // rows,
    )(cosine_multiplier, logit_bias, zq, far1, gq, token)
    return call(
        last_kernel,
        (pltpu.HBM((rows, width), BF16),) * 2,
        [SMEM] * 3 + [VMEM] * 7 + [HBM, HBM], (HBM, HBM),
        [pltpu.VMEM((rows, width), BF16), dma((rows // BLOCK,))], 12, 2 * product * rest // rows,
        input_output_aliases={10: 0, 11: 1},
    )(parity, cosine_multiplier, logit_bias, zq, far2, gq, raw1, raw2, inv1, inv2, image_out, text_out)


def solution(mesh):
    in_specs = (P("dp", None), P("dp", None), P(), P())
    out_specs = (P("dp", None), P("dp", None))
    return jax.shard_map(
        on_device, mesh=mesh, in_specs=in_specs, out_specs=out_specs, check_vma=False
    )
```

```python
import functools

import jax
import jax.numpy as jnp
from jax import lax
from jax.experimental import pallas as pl
from jax.experimental.pallas import tpu as pltpu
from jax.sharding import PartitionSpec as P

epsilon = 1e-06
LOG2_E = 1.4426950408889634
F32, BF16 = jnp.float32, jnp.bfloat16
BLOCK = 256
FIRST = 768
MIB = 2**20

VMEM = pl.BlockSpec(memory_space=pltpu.VMEM)
SMEM = pl.BlockSpec(memory_space=pltpu.SMEM)
HBM = pl.BlockSpec(memory_space=pl.ANY)


def rows_dot_rows(a, b):
    return lax.dot_general(a, b, (((1,), (1,)), ((), ())), preferred_element_type=F32)


def columns_dot(a, b):
    return lax.dot_general(a, b, (((0,), (0,)), ((), ())), preferred_element_type=F32)


def dot(a, b):
    return jnp.dot(a, b, preferred_element_type=F32)


def blocks(rows):
    return [slice(start, start + BLOCK) for start in range(0, rows, BLOCK)]


def fetch(parity, if_even, if_odd, start, target, sems):
    for i, here in enumerate(blocks(target.shape[0])):
        there = pl.ds(start + here.start, BLOCK)

        @pl.when(parity == 0)
        def _():
            pltpu.make_async_copy(if_even.at[there], target.at[here], sems.at[i]).start()

        @pl.when(parity == 1)
        def _():
            pltpu.make_async_copy(if_odd.at[there], target.at[here], sems.at[i]).start()


def arrived(source, target, sems, i, here):
    pltpu.make_async_copy(source.at[pl.ds(0, BLOCK)], target.at[here], sems.at[i]).wait()


def normalize_block(raw):
    floats = raw.astype(F32)
    inverse = lax.rsqrt(jnp.sum(floats * floats, axis=-1, keepdims=True) + epsilon)
    return (floats * inverse).astype(BF16), inverse


def first_kernel(parity_ref, image, text, z1, raw1, inv1, sems):
    fetch(parity_ref[0], image, text, 0, raw1, sems)
    for i, here in enumerate(blocks(raw1.shape[0])):
        arrived(image, raw1, sems, i, here)
        z1[here, :], inv1[here, :] = normalize_block(raw1[here, :])


def rest_kernel(
    parity_ref, image, text, z1, zp, z2, zq, rawp, raw2, invp, inv2, semsp, sems2
):
    first = z1.shape[0]
    fetch(parity_ref[0], text, image, 0, rawp, semsp)
    fetch(parity_ref[0], image, text, first, raw2, sems2)
    for i, here in enumerate(blocks(rawp.shape[0])):
        arrived(image, rawp, semsp, i, here)
        zp[here, :], invp[here, :] = normalize_block(rawp[here, :])
    zq[:first, :] = z1[...]
    for i, here in enumerate(blocks(raw2.shape[0])):
        arrived(image, raw2, sems2, i, here)
        normed, inv2[here, :] = normalize_block(raw2[here, :])
        z2[here, :] = normed
        zq[pl.ds(first + here.start, BLOCK), :] = normed


def exponential(agreement, scale, shift):
    return jnp.exp2(agreement * scale + shift)


def local_kernel(multiplier_ref, bias_ref, zp, zq, coef, gq):
    multiplier = multiplier_ref[0]
    scale, shift = -multiplier * LOG2_E, -bias_ref[0] * LOG2_E
    count = zq.shape[0]
    for here in blocks(zp.shape[0]):
        power = exponential(rows_dot_rows(zp[here, :], zq[...]), scale, shift)
        value = multiplier / (1.0 + power)
        row = lax.broadcasted_iota(jnp.int32, (BLOCK, count), 0) + here.start
        column = lax.broadcasted_iota(jnp.int32, (BLOCK, count), 1)
        coef[here, :] = jnp.where(row == column, -power * value, value).astype(BF16)
    for here in blocks(count):
        gq[here, :] = columns_dot(coef[:, here], zp[...])


def remote_coef(own, other, multiplier, scale, shift):
    power = exponential(rows_dot_rows(own, other), scale, shift)
    return (multiplier / (1.0 + power)).astype(BF16)


def backward_block(raw, inverse, upstream):
    floats = raw.astype(F32)
    inner = jnp.sum(floats * upstream, axis=-1, keepdims=True)
    return (inverse * (upstream - floats * (inverse * inverse * inner))).astype(BF16)


def put(parity, if_even, if_odd, there, source, sem):
    @pl.when(parity == 0)
    def _():
        pltpu.make_async_copy(source, if_even.at[there], sem).start()

    @pl.when(parity == 1)
    def _():
        pltpu.make_async_copy(source, if_odd.at[there], sem).start()


def near_kernel(
    parity_ref, multiplier_ref, bias_ref, zp, zq, coef, other, rawp, invp, image_out, text_out, token, held, sems
):
    token[...] = jnp.zeros_like(token)
    multiplier = multiplier_ref[0]
    scale, shift = -multiplier * LOG2_E, -bias_ref[0] * LOG2_E
    for i, here in enumerate(blocks(zp.shape[0])):
        factors = remote_coef(zp[here, :], other[...], multiplier, scale, shift)
        total = dot(coef[here, :], zq[...]) + dot(factors, other[...])
        held[here, :] = backward_block(rawp[here, :], invp[here, :], total)
        put(parity_ref[0], text_out, image_out, here, held.at[here], sems.at[i])
    for i, here in enumerate(blocks(zp.shape[0])):
        pltpu.make_async_copy(held.at[here], image_out.at[here], sems.at[i]).wait()


def far_kernel(multiplier_ref, bias_ref, zq, other, gq, after_near, total):
    multiplier = multiplier_ref[0]
    scale, shift = -multiplier * LOG2_E, -bias_ref[0] * LOG2_E
    for here in blocks(zq.shape[0]):
        factors = remote_coef(zq[here, :], other[...], multiplier, scale, shift)
        total[here, :] = gq[here, :] + dot(factors, other[...])


def last_kernel(
    parity_ref, multiplier_ref, bias_ref, zq, other, gq, raw1, raw2, inv1, inv2, image_in, text_in, image_out, text_out, held, sems
):
    multiplier = multiplier_ref[0]
    scale, shift = -multiplier * LOG2_E, -bias_ref[0] * LOG2_E
    first = raw1.shape[0]
    for i, here in enumerate(blocks(zq.shape[0])):
        factors = remote_coef(zq[here, :], other[...], multiplier, scale, shift)
        total = gq[here, :] + dot(factors, other[...])
        if here.start < first:
            raw, inverse = raw1[here, :], inv1[here, :]
        else:
            there = slice(here.start - first, here.stop - first)
            raw, inverse = raw2[there, :], inv2[there, :]
        held[here, :] = backward_block(raw, inverse, total)
        put(parity_ref[0], image_out, text_out, here, held.at[here], sems.at[i])
    for i, here in enumerate(blocks(zq.shape[0])):
        pltpu.make_async_copy(held.at[here], image_out.at[here], sems.at[i]).wait()


def shape(rows, columns, kind):
    return jax.ShapeDtypeStruct((rows, columns), kind)


def call(kernel, out_shape, in_specs, out_specs, scratch, limit, flops, **more):
    return pl.pallas_call(
        kernel,
        out_shape=out_shape,
        in_specs=in_specs,
        out_specs=out_specs,
        scratch_shapes=scratch,
        compiler_params=pltpu.CompilerParams(vmem_limit_bytes=limit * MIB),
        cost_estimate=pl.CostEstimate(flops=flops * 16 if kernel in (first_kernel, rest_kernel, local_kernel) else flops, bytes_accessed=flops, transcendentals=0),
        **more,
    )


def on_device(image_emb, text_emb, cosine_multiplier, logit_bias):
    rows, width = image_emb.shape
    count = lax.axis_size("dp")
    parity = (lax.axis_index("dp") % 2).astype(jnp.int32).reshape(1)
    near = [(e, e ^ 1) for e in range(count)]
    far = [(e, (e - 1) % count if e % 2 == 0 else (e + 1) % count) for e in range(count)]
    first, rest = FIRST, rows - FIRST
    image_emb = pltpu.with_memory_space_constraint(image_emb, pltpu.HBM)
    text_emb = pltpu.with_memory_space_constraint(text_emb, pltpu.HBM)
    dma = pltpu.SemaphoreType.DMA
    product = 2 * rows * rows * width

    z1, raw1, inv1 = call(
        first_kernel,
        (shape(first, width, BF16), shape(first, width, BF16), shape(first, 1, F32)),
        [SMEM, HBM, HBM], (VMEM,) * 3, [dma((first // BLOCK,))], 4, product // 8,
    )(parity, image_emb, text_emb)
    far1 = lax.ppermute(z1, "dp", far)
    zp, z2, zq, rawp, raw2, invp, inv2 = call(
        rest_kernel,
        (
            shape(rows, width, BF16), shape(rest, width, BF16), shape(rows, width, BF16),
            shape(rows, width, BF16), shape(rest, width, BF16), shape(rows, 1, F32), shape(rest, 1, F32),
        ),
        [SMEM, HBM, HBM, VMEM], (VMEM,) * 7, [dma((rows // BLOCK,)), dma((rest // BLOCK,))], 4, product // 4,
    )(parity, image_emb, text_emb, z1)
    near_block = lax.ppermute(zp, "dp", near)
    far2 = lax.ppermute(z2, "dp", far)
    coef, gq = call(
        local_kernel,
        (shape(rows, rows, BF16), shape(rows, width, F32)),
        [SMEM, SMEM, VMEM, VMEM], (VMEM,) * 2, [], 8, 2 * product,
    )(cosine_multiplier, logit_bias, zp, zq)
    image_out, text_out, token = call(
        near_kernel,
        (pltpu.HBM((rows, width), BF16),) * 2 + (shape(8, 128, F32),),
        [SMEM] * 3 + [VMEM] * 6, (HBM, HBM, VMEM),
        [pltpu.VMEM((rows, width), BF16), dma((rows // BLOCK,))], 12, 3 * product,
    )(parity, cosine_multiplier, logit_bias, zp, zq, coef, near_block, rawp, invp)
    gq = call(
        far_kernel, shape(rows, width, F32),
        [SMEM, SMEM, VMEM, VMEM, VMEM, VMEM], VMEM, [], 8, 2 * product * first // rows,
    )(cosine_multiplier, logit_bias, zq, far1, gq, token)
    return call(
        last_kernel,
        (pltpu.HBM((rows, width), BF16),) * 2,
        [SMEM] * 3 + [VMEM] * 7 + [HBM, HBM], (HBM, HBM),
        [pltpu.VMEM((rows, width), BF16), dma((rows // BLOCK,))], 12, 2 * product * rest // rows,
        input_output_aliases={10: 0, 11: 1},
    )(parity, cosine_multiplier, logit_bias, zq, far2, gq, raw1, raw2, inv1, inv2, image_out, text_out)


def solution(mesh):
    in_specs = (P("dp", None), P("dp", None), P(), P())
    out_specs = (P("dp", None), P("dp", None))
    return jax.shard_map(
        on_device, mesh=mesh, in_specs=in_specs, out_specs=out_specs, check_vma=False
    )
```

```python
import functools

import jax
import jax.numpy as jnp
from jax import lax
from jax.experimental import pallas as pl
from jax.experimental.pallas import tpu as pltpu
from jax.sharding import PartitionSpec as P

epsilon = 1e-06
LOG2_E = 1.4426950408889634
F32, BF16 = jnp.float32, jnp.bfloat16
BLOCK = 256
FIRST = 768
MIB = 2**20

VMEM = pl.BlockSpec(memory_space=pltpu.VMEM)
SMEM = pl.BlockSpec(memory_space=pltpu.SMEM)
HBM = pl.BlockSpec(memory_space=pl.ANY)


def rows_dot_rows(a, b):
    return lax.dot_general(a, b, (((1,), (1,)), ((), ())), preferred_element_type=F32)


def columns_dot(a, b):
    return lax.dot_general(a, b, (((0,), (0,)), ((), ())), preferred_element_type=F32)


def dot(a, b):
    return jnp.dot(a, b, preferred_element_type=F32)


def blocks(rows):
    return [slice(start, start + BLOCK) for start in range(0, rows, BLOCK)]


def fetch(parity, if_even, if_odd, start, target, sems):
    for i, here in enumerate(blocks(target.shape[0])):
        there = pl.ds(start + here.start, BLOCK)

        @pl.when(parity == 0)
        def _():
            pltpu.make_async_copy(if_even.at[there], target.at[here], sems.at[i]).start()

        @pl.when(parity == 1)
        def _():
            pltpu.make_async_copy(if_odd.at[there], target.at[here], sems.at[i]).start()


def arrived(source, target, sems, i, here):
    pltpu.make_async_copy(source.at[pl.ds(0, BLOCK)], target.at[here], sems.at[i]).wait()


def normalize_block(raw):
    floats = raw.astype(F32)
    inverse = lax.rsqrt(jnp.sum(floats * floats, axis=-1, keepdims=True) + epsilon)
    return (floats * inverse).astype(BF16), inverse


def my_parity():
    return lax.rem(lax.axis_index("dp"), 2)


def first_kernel(image, text, z1, raw1, inv1, sems):
    fetch(my_parity(), image, text, 0, raw1, sems)
    for i, here in enumerate(blocks(raw1.shape[0])):
        arrived(image, raw1, sems, i, here)
        z1[here, :], inv1[here, :] = normalize_block(raw1[here, :])


def rest_kernel(
    image, text, multiplier, bias, z1, zp, z2, zq, rawp, raw2, invp, inv2, consts, semsp, sems2
):
    first = z1.shape[0]
    parity = my_parity()
    fetch(parity, text, image, 0, rawp, semsp)
    fetch(parity, image, text, first, raw2, sems2)
    consts[0:1, :] = jnp.broadcast_to(multiplier[...], (1, consts.shape[1]))
    consts[1:2, :] = jnp.broadcast_to(bias[...], (1, consts.shape[1]))
    zq[:first, :] = z1[...]
    for i, here in enumerate(blocks(rawp.shape[0])):
        arrived(image, rawp, semsp, i, here)
        zp[here, :], invp[here, :] = normalize_block(rawp[here, :])
    for i, here in enumerate(blocks(raw2.shape[0])):
        arrived(image, raw2, sems2, i, here)
        normed, inv2[here, :] = normalize_block(raw2[here, :])
        z2[here, :] = normed
        zq[pl.ds(first + here.start, BLOCK), :] = normed


def constants(consts):
    multiplier, bias = consts[0:1, 0:1], consts[1:2, 0:1]
    return multiplier, -multiplier * LOG2_E, -bias * LOG2_E


def exponential(agreement, scale, shift):
    return jnp.exp2(agreement * scale + shift)


def local_kernel(consts, zp, zq, coef, gq):
    multiplier, scale, shift = constants(consts)
    count = zq.shape[0]
    for here in blocks(zp.shape[0]):
        power = exponential(rows_dot_rows(zp[here, :], zq[...]), scale, shift)
        value = multiplier / (1.0 + power)
        row = lax.broadcasted_iota(jnp.int32, (BLOCK, count), 0) + here.start
        column = lax.broadcasted_iota(jnp.int32, (BLOCK, count), 1)
        coef[here, :] = jnp.where(row == column, -power * value, value).astype(BF16)
    for here in blocks(count):
        gq[here, :] = columns_dot(coef[:, here], zp[...])


def backward(raw, inverse, upstream):
    floats = raw.astype(F32)
    inner = jnp.sum(floats * upstream, axis=-1, keepdims=True)
    return inverse * (upstream - floats * (inverse * inverse * inner))


def near_kernel(consts, zp, zq, coef, other, rawp, invp, grad):
    multiplier, scale, shift = constants(consts)
    for here in blocks(zp.shape[0]):
        total = dot(coef[here, :], zq[...])
        power = exponential(rows_dot_rows(zp[here, :], other[...]), scale, shift)
        factors = (multiplier / (1.0 + power)).astype(BF16)
        total = total + dot(factors, other[...])
        grad[here, :] = backward(rawp[here, :], invp[here, :], total).astype(BF16)


def put(parity, if_even, if_odd, there, source, sem):
    @pl.when(parity == 0)
    def _():
        pltpu.make_async_copy(source, if_even.at[there], sem).start()

    @pl.when(parity == 1)
    def _():
        pltpu.make_async_copy(source, if_odd.at[there], sem).start()


def raw_block(here, raw1, raw2, inv1, inv2):
    first = raw1.shape[0]
    if here.start < first:
        return raw1[here, :], inv1[here, :]
    there = slice(here.start - first, here.stop - first)
    return raw2[there, :], inv2[there, :]


def far_kernel(
    consts, zq, other, gq, raw1, raw2, inv1, inv2, after_near, so_far
):
    multiplier, scale, shift = constants(consts)
    for here in blocks(zq.shape[0]):
        power = exponential(rows_dot_rows(zq[here, :], other[...]), scale, shift)
        factors = (multiplier / (1.0 + power)).astype(BF16)
        total = gq[here, :] + dot(factors, other[...])
        so_far[here, :] = backward(*raw_block(here, raw1, raw2, inv1, inv2), total)


def last_kernel(
    consts, zq, other, so_far, raw1, raw2, inv1, inv2, grad, image_out, text_out, held, sems, grad_sem
):
    multiplier, scale, shift = constants(consts)
    parity = my_parity()
    everything = pl.ds(0, grad.shape[0])
    put(parity, text_out, image_out, everything, grad, grad_sem)
    pieces = blocks(zq.shape[0])
    ahead = rows_dot_rows(zq[pieces[0], :], other[...])
    for i, here in enumerate(pieces):
        agreement = ahead
        if i + 1 < len(pieces):
            ahead = rows_dot_rows(zq[pieces[i + 1], :], other[...])
        factors = multiplier / (1.0 + exponential(agreement, scale, shift))
        inner = jnp.sum(factors * agreement, axis=-1, keepdims=True)
        term = dot(factors.astype(BF16), other[...])
        raw, inverse = raw_block(here, raw1, raw2, inv1, inv2)
        more = inverse * term - raw.astype(F32) * (inverse * inverse * inner)
        held[here, :] = (so_far[here, :] + more).astype(BF16)
        put(parity, image_out, text_out, here, held.at[here], sems.at[i])
    pltpu.make_async_copy(grad, image_out.at[everything], grad_sem).wait()
    for i, here in enumerate(pieces):
        pltpu.make_async_copy(held.at[here], image_out.at[here], sems.at[i]).wait()


def shape(rows, columns, kind):
    return jax.ShapeDtypeStruct((rows, columns), kind)


def call(kernel, out_shape, in_specs, out_specs, scratch, limit, flops, weight=1, **more):
    return pl.pallas_call(
        kernel,
        out_shape=out_shape,
        in_specs=in_specs,
        out_specs=out_specs,
        scratch_shapes=scratch,
        compiler_params=pltpu.CompilerParams(vmem_limit_bytes=limit * MIB),
        cost_estimate=pl.CostEstimate(
            flops=flops * weight, bytes_accessed=flops, transcendentals=0
        ),
        **more,
    )


def on_device(image_emb, text_emb, cosine_multiplier, logit_bias):
    rows, width = image_emb.shape
    count = lax.axis_size("dp")
    near = [(e, e ^ 1) for e in range(count)]
    far = [(e, (e - 1) % count if e % 2 == 0 else (e + 1) % count) for e in range(count)]
    first, rest = FIRST, rows - FIRST
    image_emb = pltpu.with_memory_space_constraint(image_emb, pltpu.HBM)
    text_emb = pltpu.with_memory_space_constraint(text_emb, pltpu.HBM)
    dma = pltpu.SemaphoreType.DMA
    product = 2 * rows * rows * width

    z1, raw1, inv1 = call(
        first_kernel,
        (shape(first, width, BF16), shape(first, width, BF16), shape(first, 1, F32)),
        [HBM, HBM], (VMEM,) * 3, [dma((first // BLOCK,))], 4, product // 8, 16,
    )(image_emb, text_emb)
    far1 = lax.ppermute(z1, "dp", far)
    zp, z2, zq, rawp, raw2, invp, inv2, consts = call(
        rest_kernel,
        (
            shape(rows, width, BF16), shape(rest, width, BF16), shape(rows, width, BF16),
            shape(rows, width, BF16), shape(rest, width, BF16), shape(rows, 1, F32), shape(rest, 1, F32),
            shape(8, 128, F32),
        ),
        [HBM] * 2 + [VMEM] * 3, (VMEM,) * 8,
        [dma((rows // BLOCK,)), dma((rest // BLOCK,))], 4, product // 4, 16,
    )(image_emb, text_emb, cosine_multiplier.reshape(1, 1), logit_bias.reshape(1, 1), z1)
    near_block = lax.ppermute(zp, "dp", near)
    far2 = lax.ppermute(z2, "dp", far)
    coef, gq = call(
        local_kernel,
        (shape(rows, rows, BF16), shape(rows, width, F32)),
        [VMEM] * 3, (VMEM,) * 2, [], 8, 2 * product, 16,
    )(consts, zp, zq)
    grad = call(
        near_kernel, shape(rows, width, BF16),
        [VMEM] * 7, VMEM, [], 12, 3 * product,
    )(consts, zp, zq, coef, near_block, rawp, invp)
    so_far = call(
        far_kernel, shape(rows, width, F32),
        [VMEM] * 9, VMEM, [], 8, 2 * product * first // rows,
    )(consts, zq, far1, gq, raw1, raw2, inv1, inv2, grad)
    return call(
        last_kernel,
        (pltpu.HBM((rows, width), BF16),) * 2,
        [VMEM] * 9, (HBM, HBM),
        [pltpu.VMEM((rows, width), BF16), dma((rows // BLOCK,)), dma], 12, 2 * product * rest // rows,
    )(consts, zq, far2, so_far, raw1, raw2, inv1, inv2, grad)


def solution(mesh):
    in_specs = (P("dp", None), P("dp", None), P(), P())
    out_specs = (P("dp", None), P("dp", None))
    return jax.shard_map(
        on_device, mesh=mesh, in_specs=in_specs, out_specs=out_specs, check_vma=False
    )
```

```python
import functools

import jax
import jax.numpy as jnp
from jax import lax
from jax.experimental import pallas as pl
from jax.experimental.pallas import tpu as pltpu
from jax.sharding import PartitionSpec as P

epsilon = 1e-06
LOG2_E = 1.4426950408889634
F32, BF16 = jnp.float32, jnp.bfloat16
BLOCK = 256
FIRST = 768
MIB = 2**20

VMEM = pl.BlockSpec(memory_space=pltpu.VMEM)
SMEM = pl.BlockSpec(memory_space=pltpu.SMEM)
HBM = pl.BlockSpec(memory_space=pl.ANY)


def rows_dot_rows(a, b):
    return lax.dot_general(a, b, (((1,), (1,)), ((), ())), preferred_element_type=F32)


def columns_dot(a, b):
    return lax.dot_general(a, b, (((0,), (0,)), ((), ())), preferred_element_type=F32)


def dot(a, b):
    return jnp.dot(a, b, preferred_element_type=F32)


def blocks(rows):
    return [slice(start, start + BLOCK) for start in range(0, rows, BLOCK)]


def fetch(parity, if_even, if_odd, start, target, sems):
    for i, here in enumerate(blocks(target.shape[0])):
        there = pl.ds(start + here.start, BLOCK)

        @pl.when(parity == 0)
        def _():
            pltpu.make_async_copy(if_even.at[there], target.at[here], sems.at[i]).start()

        @pl.when(parity == 1)
        def _():
            pltpu.make_async_copy(if_odd.at[there], target.at[here], sems.at[i]).start()


def arrived(source, target, sems, i, here):
    pltpu.make_async_copy(source.at[pl.ds(0, BLOCK)], target.at[here], sems.at[i]).wait()


def normalize_block(raw):
    floats = raw.astype(F32)
    inverse = lax.rsqrt(jnp.sum(floats * floats, axis=-1, keepdims=True) + epsilon)
    return (floats * inverse).astype(BF16), inverse


def length_ratio(normed, inverse):
    floats = normed.astype(F32)
    squares = jnp.sum(floats * floats, axis=-1, keepdims=True) + 1e-30
    return 0.5 + 0.5 * (1.0 - epsilon * inverse * inverse) / squares


def my_parity():
    return lax.rem(lax.axis_index("dp"), 2)


def first_kernel(image, text, z1, raw1, inv1, sems):
    fetch(my_parity(), image, text, 0, raw1, sems)
    for i, here in enumerate(blocks(raw1.shape[0])):
        arrived(image, raw1, sems, i, here)
        z1[here, :], inv1[here, :] = normalize_block(raw1[here, :])


def rest_kernel(
    image, text, multiplier, bias, z1, inv1, zp, z2, zq, rawp, raw2, invp, inv2, consts, ratio, semsp, sems2
):
    first = z1.shape[0]
    parity = my_parity()
    fetch(parity, text, image, 0, rawp, semsp)
    fetch(parity, image, text, first, raw2, sems2)
    consts[0:1, :] = jnp.broadcast_to(multiplier[...], (1, consts.shape[1]))
    consts[1:2, :] = jnp.broadcast_to(bias[...], (1, consts.shape[1]))
    for here in blocks(first):
        zq[here, :] = z1[here, :]
        ratio[here, :] = length_ratio(z1[here, :], inv1[here, :])
    for i, here in enumerate(blocks(rawp.shape[0])):
        arrived(image, rawp, semsp, i, here)
        zp[here, :], invp[here, :] = normalize_block(rawp[here, :])
    for i, here in enumerate(blocks(raw2.shape[0])):
        arrived(image, raw2, sems2, i, here)
        normed, inverse = normalize_block(raw2[here, :])
        z2[here, :], inv2[here, :] = normed, inverse
        there = slice(first + here.start, first + here.stop)
        zq[there, :] = normed
        ratio[there, :] = length_ratio(normed, inverse)


def constants(consts):
    multiplier, bias = consts[0:1, 0:1], consts[1:2, 0:1]
    return multiplier, -multiplier * LOG2_E, -bias * LOG2_E


def exponential(agreement, scale, shift):
    return jnp.exp2(agreement * scale + shift)


def local_kernel(consts, zp, zq, coef, gq, along):
    multiplier, scale, shift = constants(consts)
    count = zq.shape[0]
    for here in blocks(zp.shape[0]):
        power = exponential(rows_dot_rows(zp[here, :], zq[...]), scale, shift)
        value = multiplier / (1.0 + power)
        row = lax.broadcasted_iota(jnp.int32, (BLOCK, count), 0) + here.start
        column = lax.broadcasted_iota(jnp.int32, (BLOCK, count), 1)
        coef[here, :] = jnp.where(row == column, -power * value, value).astype(BF16)
    for here in blocks(count):
        total = columns_dot(coef[:, here], zp[...])
        gq[here, :] = total
        along[here, :] = jnp.sum(zq[here, :].astype(F32) * total, axis=-1, keepdims=True)


def backward(raw, inverse, upstream):
    floats = raw.astype(F32)
    inner = jnp.sum(floats * upstream, axis=-1, keepdims=True)
    return inverse * (upstream - floats * (inverse * inverse * inner))


def near_kernel(consts, zp, zq, coef, other, rawp, invp, grad):
    multiplier, scale, shift = constants(consts)
    for here in blocks(zp.shape[0]):
        total = dot(coef[here, :], zq[...])
        power = exponential(rows_dot_rows(zp[here, :], other[...]), scale, shift)
        factors = (multiplier / (1.0 + power)).astype(BF16)
        total = total + dot(factors, other[...])
        grad[here, :] = backward(rawp[here, :], invp[here, :], total).astype(BF16)


def put(parity, if_even, if_odd, there, source, sem):
    @pl.when(parity == 0)
    def _():
        pltpu.make_async_copy(source, if_even.at[there], sem).start()

    @pl.when(parity == 1)
    def _():
        pltpu.make_async_copy(source, if_odd.at[there], sem).start()


def raw_block(here, raw1, raw2, inv1, inv2):
    first = raw1.shape[0]
    if here.start < first:
        return raw1[here, :], inv1[here, :]
    there = slice(here.start - first, here.stop - first)
    return raw2[there, :], inv2[there, :]


def far_terms(consts, zq, other):
    multiplier, scale, shift = constants(consts)
    pieces = blocks(zq.shape[0])
    ahead = rows_dot_rows(zq[pieces[0], :], other[...])
    for i, here in enumerate(pieces):
        agreement = ahead
        if i + 1 < len(pieces):
            ahead = rows_dot_rows(zq[pieces[i + 1], :], other[...])
        factors = multiplier / (1.0 + exponential(agreement, scale, shift))
        along = jnp.sum(factors * agreement, axis=-1, keepdims=True)
        yield i, here, dot(factors.astype(BF16), other[...]), along


def far_kernel(consts, zq, other, gq, along_in, after_near, so_far, along_out):
    for _, here, term, along in far_terms(consts, zq, other):
        so_far[here, :] = gq[here, :] + term
        along_out[here, :] = along_in[here, :] + along


def last_kernel(
    consts, zq, other, so_far, along_in, ratio, raw1, raw2, inv1, inv2, grad, image_out, text_out, held, sems, grad_sem
):
    parity = my_parity()
    everything = pl.ds(0, grad.shape[0])
    put(parity, text_out, image_out, everything, grad, grad_sem)
    for i, here, term, along in far_terms(consts, zq, other):
        raw, inverse = raw_block(here, raw1, raw2, inv1, inv2)
        inner = ratio[here, :] * (along_in[here, :] + along)
        total = so_far[here, :] + term
        held[here, :] = (inverse * total - raw.astype(F32) * (inverse * inverse * inner)).astype(BF16)
        put(parity, image_out, text_out, here, held.at[here], sems.at[i])
    pltpu.make_async_copy(grad, image_out.at[everything], grad_sem).wait()
    for i, here in enumerate(blocks(zq.shape[0])):
        pltpu.make_async_copy(held.at[here], image_out.at[here], sems.at[i]).wait()


def shape(rows, columns, kind):
    return jax.ShapeDtypeStruct((rows, columns), kind)


def call(kernel, out_shape, in_specs, out_specs, scratch, limit, flops, weight=1, **more):
    return pl.pallas_call(
        kernel,
        out_shape=out_shape,
        in_specs=in_specs,
        out_specs=out_specs,
        scratch_shapes=scratch,
        compiler_params=pltpu.CompilerParams(vmem_limit_bytes=limit * MIB),
        cost_estimate=pl.CostEstimate(
            flops=flops * weight, bytes_accessed=flops, transcendentals=0
        ),
        **more,
    )


def on_device(image_emb, text_emb, cosine_multiplier, logit_bias):
    rows, width = image_emb.shape
    count = lax.axis_size("dp")
    near = [(e, e ^ 1) for e in range(count)]
    far = [(e, (e - 1) % count if e % 2 == 0 else (e + 1) % count) for e in range(count)]
    first, rest = FIRST, rows - FIRST
    image_emb = pltpu.with_memory_space_constraint(image_emb, pltpu.HBM)
    text_emb = pltpu.with_memory_space_constraint(text_emb, pltpu.HBM)
    dma = pltpu.SemaphoreType.DMA
    product = 2 * rows * rows * width

    z1, raw1, inv1 = call(
        first_kernel,
        (shape(first, width, BF16), shape(first, width, BF16), shape(first, 1, F32)),
        [HBM, HBM], (VMEM,) * 3, [dma((first // BLOCK,))], 4, product // 8, 16,
    )(image_emb, text_emb)
    far1 = lax.ppermute(z1, "dp", far)
    zp, z2, zq, rawp, raw2, invp, inv2, consts, ratio = call(
        rest_kernel,
        (
            shape(rows, width, BF16), shape(rest, width, BF16), shape(rows, width, BF16),
            shape(rows, width, BF16), shape(rest, width, BF16), shape(rows, 1, F32), shape(rest, 1, F32),
            shape(8, 128, F32), shape(rows, 1, F32),
        ),
        [HBM] * 2 + [VMEM] * 4, (VMEM,) * 9,
        [dma((rows // BLOCK,)), dma((rest // BLOCK,))], 4, product // 4, 16,
    )(image_emb, text_emb, cosine_multiplier.reshape(1, 1), logit_bias.reshape(1, 1), z1, inv1)
    near_block = lax.ppermute(zp, "dp", near)
    far2 = lax.ppermute(z2, "dp", far)
    coef, gq, along = call(
        local_kernel,
        (shape(rows, rows, BF16), shape(rows, width, F32), shape(rows, 1, F32)),
        [VMEM] * 3, (VMEM,) * 3, [], 8, 2 * product, 16,
    )(consts, zp, zq)
    grad = call(
        near_kernel, shape(rows, width, BF16),
        [VMEM] * 7, VMEM, [], 12, 3 * product,
    )(consts, zp, zq, coef, near_block, rawp, invp)
    so_far, along = call(
        far_kernel, (shape(rows, width, F32), shape(rows, 1, F32)),
        [VMEM] * 6, (VMEM,) * 2, [], 8, 2 * product * first // rows,
    )(consts, zq, far1, gq, along, grad)
    return call(
        last_kernel,
        (pltpu.HBM((rows, width), BF16),) * 2,
        [VMEM] * 11, (HBM, HBM),
        [pltpu.VMEM((rows, width), BF16), dma((rows // BLOCK,)), dma], 12, 2 * product * rest // rows,
    )(consts, zq, far2, so_far, along, ratio, raw1, raw2, inv1, inv2, grad)


def solution(mesh):
    in_specs = (P("dp", None), P("dp", None), P(), P())
    out_specs = (P("dp", None), P("dp", None))
    return jax.shard_map(
        on_device, mesh=mesh, in_specs=in_specs, out_specs=out_specs, check_vma=False
    )
```

```python
import functools

import jax
import jax.numpy as jnp
from jax import lax
from jax.experimental import pallas as pl
from jax.experimental.pallas import tpu as pltpu
from jax.sharding import PartitionSpec as P

epsilon = 1e-06
LOG2_E = 1.4426950408889634
F32, BF16 = jnp.float32, jnp.bfloat16
BLOCK = 256
HALF = BLOCK // 2
FIRST = 768
MIB = 2**20

VMEM = pl.BlockSpec(memory_space=pltpu.VMEM)
SMEM = pl.BlockSpec(memory_space=pltpu.SMEM)
HBM = pl.BlockSpec(memory_space=pl.ANY)


def rows_dot_rows(a, b):
    return lax.dot_general(a, b, (((1,), (1,)), ((), ())), preferred_element_type=F32)


def columns_dot(a, b):
    return lax.dot_general(a, b, (((0,), (0,)), ((), ())), preferred_element_type=F32)


def dot(a, b):
    return jnp.dot(a, b, preferred_element_type=F32)


def blocks(rows):
    return [slice(start, start + BLOCK) for start in range(0, rows, BLOCK)]


def fetch(parity, if_even, if_odd, start, target, sems):
    for i, here in enumerate(blocks(target.shape[0])):
        there = pl.ds(start + here.start, BLOCK)

        @pl.when(parity == 0)
        def _():
            pltpu.make_async_copy(if_even.at[there], target.at[here], sems.at[i]).start()

        @pl.when(parity == 1)
        def _():
            pltpu.make_async_copy(if_odd.at[there], target.at[here], sems.at[i]).start()


def arrived(source, target, sems, i, here):
    pltpu.make_async_copy(source.at[pl.ds(0, BLOCK)], target.at[here], sems.at[i]).wait()


def normalize_block(raw):
    floats = raw.astype(F32)
    inverse = lax.rsqrt(jnp.sum(floats * floats, axis=-1, keepdims=True) + epsilon)
    return (floats * inverse).astype(BF16), inverse


def my_parity():
    return lax.rem(lax.axis_index("dp"), 2)


def first_kernel(image, text, z1, raw1, inv1, sems):
    fetch(my_parity(), image, text, 0, raw1, sems)
    for i, here in enumerate(blocks(raw1.shape[0])):
        arrived(image, raw1, sems, i, here)
        z1[here, :], inv1[here, :] = normalize_block(raw1[here, :])


def rest_kernel(
    image, text, multiplier, bias, z1, zp, z2, zq, rawp, raw2, invp, inv2, consts, semsp, sems2
):
    first = z1.shape[0]
    parity = my_parity()
    fetch(parity, text, image, 0, rawp, semsp)
    fetch(parity, image, text, first, raw2, sems2)
    consts[0:1, :] = jnp.broadcast_to(multiplier[...], (1, consts.shape[1]))
    consts[1:2, :] = jnp.broadcast_to(bias[...], (1, consts.shape[1]))
    zq[:first, :] = z1[...]
    for i, here in enumerate(blocks(rawp.shape[0])):
        arrived(image, rawp, semsp, i, here)
        zp[here, :], invp[here, :] = normalize_block(rawp[here, :])
    for i, here in enumerate(blocks(raw2.shape[0])):
        arrived(image, raw2, sems2, i, here)
        normed, inv2[here, :] = normalize_block(raw2[here, :])
        z2[here, :] = normed
        zq[pl.ds(first + here.start, BLOCK), :] = normed


def constants(consts):
    multiplier, bias = consts[0:1, 0:1], consts[1:2, 0:1]
    return multiplier, -multiplier * LOG2_E, -bias * LOG2_E


def exponential(agreement, scale, shift):
    return jnp.exp2(agreement * scale + shift)


def local_kernel(consts, zp, zq, coef, gq):
    multiplier, scale, shift = constants(consts)
    count = zq.shape[0]
    for here in blocks(zp.shape[0]):
        power = exponential(rows_dot_rows(zp[here, :], zq[...]), scale, shift)
        value = multiplier / (1.0 + power)
        row = lax.broadcasted_iota(jnp.int32, (BLOCK, count), 0) + here.start
        column = lax.broadcasted_iota(jnp.int32, (BLOCK, count), 1)
        coef[here, :] = jnp.where(row == column, -power * value, value).astype(BF16)
    for here in blocks(count):
        gq[here, :] = columns_dot(coef[:, here], zp[...])


def backward(raw, inverse, upstream):
    floats = raw.astype(F32)
    inner = jnp.sum(floats * upstream, axis=-1, keepdims=True)
    return inverse * (upstream - floats * (inverse * inverse * inner))


def near_kernel(consts, zp, zq, coef, other, rawp, invp, grad):
    multiplier, scale, shift = constants(consts)
    for here in blocks(zp.shape[0]):
        total = dot(coef[here, :], zq[...])
        power = exponential(rows_dot_rows(zp[here, :], other[...]), scale, shift)
        factors = (multiplier / (1.0 + power)).astype(BF16)
        total = total + dot(factors, other[...])
        grad[here, :] = backward(rawp[here, :], invp[here, :], total).astype(BF16)


def put(parity, if_even, if_odd, there, source, sem):
    @pl.when(parity == 0)
    def _():
        pltpu.make_async_copy(source, if_even.at[there], sem).start()

    @pl.when(parity == 1)
    def _():
        pltpu.make_async_copy(source, if_odd.at[there], sem).start()


def raw_block(here, raw1, raw2, inv1, inv2):
    first = raw1.shape[0]
    if here.start < first:
        return raw1[here, :], inv1[here, :]
    there = slice(here.start - first, here.stop - first)
    return raw2[there, :], inv2[there, :]


def far_kernel(consts, zq, other, gq, after_near, so_far):
    multiplier, scale, shift = constants(consts)
    for here in blocks(zq.shape[0]):
        power = exponential(rows_dot_rows(zq[here, :], other[...]), scale, shift)
        factors = (multiplier / (1.0 + power)).astype(BF16)
        total = gq[here, :] + dot(factors, other[...])
        so_far[here, :] = total


def last_kernel(
    consts, zq, other, so_far, raw1, raw2, inv1, inv2, grad, image_out, text_out, held, sems, grad_sem
):
    multiplier, scale, shift = constants(consts)
    parity = my_parity()
    everything = pl.ds(0, grad.shape[0])
    put(parity, text_out, image_out, everything, grad, grad_sem)
    pieces = blocks(zq.shape[0])
    ahead = rows_dot_rows(zq[pieces[0], :], other[...])
    for i, here in enumerate(pieces):
        agreement = ahead
        if i + 1 < len(pieces):
            ahead = rows_dot_rows(zq[pieces[i + 1], :], other[...])
        factors = (multiplier / (1.0 + exponential(agreement, scale, shift))).astype(BF16)
        total = so_far[here, :] + dot(factors, other[...])
        raw, inverse = raw_block(here, raw1, raw2, inv1, inv2)
        for j in range(2):
            half = slice(j * HALF, (j + 1) * HALF)
            there = slice(here.start + half.start, here.start + half.stop)
            held[there, :] = backward(raw[half, :], inverse[half, :], total[half, :]).astype(BF16)
            put(parity, image_out, text_out, there, held.at[there], sems.at[2 * i + j])
    pltpu.make_async_copy(grad, image_out.at[everything], grad_sem).wait()
    for i in range(zq.shape[0] // HALF):
        there = pl.ds(i * HALF, HALF)
        pltpu.make_async_copy(held.at[there], image_out.at[there], sems.at[i]).wait()


def shape(rows, columns, kind):
    return jax.ShapeDtypeStruct((rows, columns), kind)


def call(kernel, out_shape, in_specs, out_specs, scratch, limit, flops, weight=1, **more):
    return pl.pallas_call(
        kernel,
        out_shape=out_shape,
        in_specs=in_specs,
        out_specs=out_specs,
        scratch_shapes=scratch,
        compiler_params=pltpu.CompilerParams(vmem_limit_bytes=limit * MIB),
        cost_estimate=pl.CostEstimate(
            flops=flops * weight, bytes_accessed=flops, transcendentals=0
        ),
        **more,
    )


def on_device(image_emb, text_emb, cosine_multiplier, logit_bias):
    rows, width = image_emb.shape
    count = lax.axis_size("dp")
    near = [(e, e ^ 1) for e in range(count)]
    far = [(e, (e - 1) % count if e % 2 == 0 else (e + 1) % count) for e in range(count)]
    first, rest = FIRST, rows - FIRST
    image_emb = pltpu.with_memory_space_constraint(image_emb, pltpu.HBM)
    text_emb = pltpu.with_memory_space_constraint(text_emb, pltpu.HBM)
    dma = pltpu.SemaphoreType.DMA
    product = 2 * rows * rows * width

    z1, raw1, inv1 = call(
        first_kernel,
        (shape(first, width, BF16), shape(first, width, BF16), shape(first, 1, F32)),
        [HBM, HBM], (VMEM,) * 3, [dma((first // BLOCK,))], 4, product // 8, 16,
    )(image_emb, text_emb)
    far1 = lax.ppermute(z1, "dp", far)
    zp, z2, zq, rawp, raw2, invp, inv2, consts = call(
        rest_kernel,
        (
            shape(rows, width, BF16), shape(rest, width, BF16), shape(rows, width, BF16),
            shape(rows, width, BF16), shape(rest, width, BF16), shape(rows, 1, F32), shape(rest, 1, F32),
            shape(8, 128, F32),
        ),
        [HBM] * 2 + [VMEM] * 3, (VMEM,) * 8,
        [dma((rows // BLOCK,)), dma((rest // BLOCK,))], 4, product // 4, 16,
    )(image_emb, text_emb, cosine_multiplier.reshape(1, 1), logit_bias.reshape(1, 1), z1)
    near_block = lax.ppermute(zp, "dp", near)
    far2 = lax.ppermute(z2, "dp", far)
    coef, gq = call(
        local_kernel,
        (shape(rows, rows, BF16), shape(rows, width, F32)),
        [VMEM] * 3, (VMEM,) * 2, [], 8, 2 * product, 16,
    )(consts, zp, zq)
    grad = call(
        near_kernel, shape(rows, width, BF16),
        [VMEM] * 7, VMEM, [], 12, 3 * product,
    )(consts, zp, zq, coef, near_block, rawp, invp)
    so_far = call(
        far_kernel, shape(rows, width, F32),
        [VMEM] * 5, VMEM, [], 8, 2 * product * first // rows,
    )(consts, zq, far1, gq, grad)
    return call(
        last_kernel,
        (pltpu.HBM((rows, width), BF16),) * 2,
        [VMEM] * 9, (HBM, HBM),
        [pltpu.VMEM((rows, width), BF16), dma((rows // HALF,)), dma], 12, 2 * product * rest // rows,
    )(consts, zq, far2, so_far, raw1, raw2, inv1, inv2, grad)


def solution(mesh):
    in_specs = (P("dp", None), P("dp", None), P(), P())
    out_specs = (P("dp", None), P("dp", None))
    return jax.shard_map(
        on_device, mesh=mesh, in_specs=in_specs, out_specs=out_specs, check_vma=False
    )
```

```python
import functools

import jax
import jax.numpy as jnp
from jax import lax
from jax.experimental import pallas as pl
from jax.experimental.pallas import tpu as pltpu
from jax.sharding import PartitionSpec as P

epsilon = 1e-06
LOG2_E = 1.4426950408889634
F32, BF16 = jnp.float32, jnp.bfloat16
BLOCK = 256
HALF = BLOCK // 2
FIRST = 768
MIB = 2**20

VMEM = pl.BlockSpec(memory_space=pltpu.VMEM)
SMEM = pl.BlockSpec(memory_space=pltpu.SMEM)
HBM = pl.BlockSpec(memory_space=pl.ANY)


def rows_dot_rows(a, b):
    return lax.dot_general(a, b, (((1,), (1,)), ((), ())), preferred_element_type=F32)


def columns_dot(a, b):
    return lax.dot_general(a, b, (((0,), (0,)), ((), ())), preferred_element_type=F32)


def dot(a, b):
    return jnp.dot(a, b, preferred_element_type=F32)


def blocks(rows):
    return [slice(start, start + BLOCK) for start in range(0, rows, BLOCK)]


def fetch(parity, if_even, if_odd, start, target, sems):
    for i, here in enumerate(blocks(target.shape[0])):
        there = pl.ds(start + here.start, BLOCK)

        @pl.when(parity == 0)
        def _():
            pltpu.make_async_copy(if_even.at[there], target.at[here], sems.at[i]).start()

        @pl.when(parity == 1)
        def _():
            pltpu.make_async_copy(if_odd.at[there], target.at[here], sems.at[i]).start()


def arrived(source, target, sems, i, here):
    pltpu.make_async_copy(source.at[pl.ds(0, BLOCK)], target.at[here], sems.at[i]).wait()


def normalize_block(raw):
    floats = raw.astype(F32)
    inverse = lax.rsqrt(jnp.sum(floats * floats, axis=-1, keepdims=True) + epsilon)
    return (floats * inverse).astype(BF16), inverse


def length_ratio(normed, inverse):
    floats = normed.astype(F32)
    squares = jnp.sum(floats * floats, axis=-1, keepdims=True) + 1e-30
    return 0.5 + 0.5 * (1.0 - epsilon * inverse * inverse) / squares


def my_parity():
    return lax.rem(lax.axis_index("dp"), 2)


def first_kernel(image, text, z1, raw1, inv1, sems):
    fetch(my_parity(), image, text, 0, raw1, sems)
    for i, here in enumerate(blocks(raw1.shape[0])):
        arrived(image, raw1, sems, i, here)
        z1[here, :], inv1[here, :] = normalize_block(raw1[here, :])


def rest_kernel(
    image, text, multiplier, bias, z1, inv1, zp, z2, zq, rawp, raw2, invp, inv2, consts, ratio, semsp, sems2
):
    first = z1.shape[0]
    parity = my_parity()
    fetch(parity, text, image, 0, rawp, semsp)
    fetch(parity, image, text, first, raw2, sems2)
    consts[0:1, :] = jnp.broadcast_to(multiplier[...], (1, consts.shape[1]))
    consts[1:2, :] = jnp.broadcast_to(bias[...], (1, consts.shape[1]))
    for here in blocks(first):
        zq[here, :] = z1[here, :]
        ratio[here, :] = length_ratio(z1[here, :], inv1[here, :])
    for i, here in enumerate(blocks(rawp.shape[0])):
        arrived(image, rawp, semsp, i, here)
        zp[here, :], invp[here, :] = normalize_block(rawp[here, :])
    for i, here in enumerate(blocks(raw2.shape[0])):
        arrived(image, raw2, sems2, i, here)
        normed, inverse = normalize_block(raw2[here, :])
        z2[here, :], inv2[here, :] = normed, inverse
        there = slice(first + here.start, first + here.stop)
        zq[there, :] = normed
        ratio[there, :] = length_ratio(normed, inverse)


def constants(consts):
    multiplier, bias = consts[0:1, 0:1], consts[1:2, 0:1]
    return multiplier, -multiplier * LOG2_E, -bias * LOG2_E


def exponential(agreement, scale, shift):
    return jnp.exp2(agreement * scale + shift)


def local_kernel(consts, zp, zq, coef, gq, along):
    multiplier, scale, shift = constants(consts)
    count = zq.shape[0]
    for here in blocks(zp.shape[0]):
        power = exponential(rows_dot_rows(zp[here, :], zq[...]), scale, shift)
        value = multiplier / (1.0 + power)
        row = lax.broadcasted_iota(jnp.int32, (BLOCK, count), 0) + here.start
        column = lax.broadcasted_iota(jnp.int32, (BLOCK, count), 1)
        coef[here, :] = jnp.where(row == column, -power * value, value).astype(BF16)
    for here in blocks(count):
        total = columns_dot(coef[:, here], zp[...])
        gq[here, :] = total
        along[here, :] = jnp.sum(zq[here, :].astype(F32) * total, axis=-1, keepdims=True)


def backward(raw, inverse, upstream):
    floats = raw.astype(F32)
    inner = jnp.sum(floats * upstream, axis=-1, keepdims=True)
    return inverse * (upstream - floats * (inverse * inverse * inner))


def near_kernel(consts, zp, zq, coef, other, rawp, invp, grad):
    multiplier, scale, shift = constants(consts)
    for here in blocks(zp.shape[0]):
        total = dot(coef[here, :], zq[...])
        power = exponential(rows_dot_rows(zp[here, :], other[...]), scale, shift)
        factors = (multiplier / (1.0 + power)).astype(BF16)
        total = total + dot(factors, other[...])
        grad[here, :] = backward(rawp[here, :], invp[here, :], total).astype(BF16)


def put(parity, if_even, if_odd, there, source, sem):
    @pl.when(parity == 0)
    def _():
        pltpu.make_async_copy(source, if_even.at[there], sem).start()

    @pl.when(parity == 1)
    def _():
        pltpu.make_async_copy(source, if_odd.at[there], sem).start()


def raw_block(here, raw1, raw2, inv1, inv2):
    first = raw1.shape[0]
    if here.start < first:
        return raw1[here, :], inv1[here, :]
    there = slice(here.start - first, here.stop - first)
    return raw2[there, :], inv2[there, :]


def far_terms(consts, zq, other):
    multiplier, scale, shift = constants(consts)
    pieces = blocks(zq.shape[0])
    ahead = rows_dot_rows(zq[pieces[0], :], other[...])
    for i, here in enumerate(pieces):
        agreement = ahead
        if i + 1 < len(pieces):
            ahead = rows_dot_rows(zq[pieces[i + 1], :], other[...])
        factors = (multiplier / (1.0 + exponential(agreement, scale, shift))).astype(BF16)
        along = jnp.sum(factors.astype(F32) * agreement, axis=-1, keepdims=True)
        yield i, here, dot(factors, other[...]), along


def far_kernel(consts, zq, other, gq, along_in, after_near, so_far, along_out):
    for _, here, term, along in far_terms(consts, zq, other):
        so_far[here, :] = gq[here, :] + term
        along_out[here, :] = along_in[here, :] + along


def last_kernel(
    consts, zq, other, so_far, along_in, ratio, raw1, raw2, inv1, inv2, grad, image_out, text_out, held, sems, grad_sem
):
    parity = my_parity()
    everything = pl.ds(0, grad.shape[0])
    put(parity, text_out, image_out, everything, grad, grad_sem)
    for i, here, term, along in far_terms(consts, zq, other):
        raw, inverse = raw_block(here, raw1, raw2, inv1, inv2)
        inner = ratio[here, :] * (along_in[here, :] + along)
        total = so_far[here, :] + term
        back = (inverse * total - raw.astype(F32) * (inverse * inverse * inner)).astype(BF16)
        for j in range(2):
            there = slice(here.start + j * HALF, here.start + (j + 1) * HALF)
            held[there, :] = back[j * HALF : (j + 1) * HALF, :]
            put(parity, image_out, text_out, there, held.at[there], sems.at[2 * i + j])
    pltpu.make_async_copy(grad, image_out.at[everything], grad_sem).wait()
    for i in range(zq.shape[0] // HALF):
        there = pl.ds(i * HALF, HALF)
        pltpu.make_async_copy(held.at[there], image_out.at[there], sems.at[i]).wait()


def shape(rows, columns, kind):
    return jax.ShapeDtypeStruct((rows, columns), kind)


def call(kernel, out_shape, in_specs, out_specs, scratch, limit, flops, weight=1, **more):
    return pl.pallas_call(
        kernel,
        out_shape=out_shape,
        in_specs=in_specs,
        out_specs=out_specs,
        scratch_shapes=scratch,
        compiler_params=pltpu.CompilerParams(vmem_limit_bytes=limit * MIB),
        cost_estimate=pl.CostEstimate(
            flops=flops * weight, bytes_accessed=flops, transcendentals=0
        ),
        **more,
    )


def on_device(image_emb, text_emb, cosine_multiplier, logit_bias):
    rows, width = image_emb.shape
    count = lax.axis_size("dp")
    near = [(e, e ^ 1) for e in range(count)]
    far = [(e, (e - 1) % count if e % 2 == 0 else (e + 1) % count) for e in range(count)]
    first, rest = FIRST, rows - FIRST
    image_emb = pltpu.with_memory_space_constraint(image_emb, pltpu.HBM)
    text_emb = pltpu.with_memory_space_constraint(text_emb, pltpu.HBM)
    dma = pltpu.SemaphoreType.DMA
    product = 2 * rows * rows * width

    z1, raw1, inv1 = call(
        first_kernel,
        (shape(first, width, BF16), shape(first, width, BF16), shape(first, 1, F32)),
        [HBM, HBM], (VMEM,) * 3, [dma((first // BLOCK,))], 4, product // 8, 16,
    )(image_emb, text_emb)
    far1 = lax.ppermute(z1, "dp", far)
    zp, z2, zq, rawp, raw2, invp, inv2, consts, ratio = call(
        rest_kernel,
        (
            shape(rows, width, BF16), shape(rest, width, BF16), shape(rows, width, BF16),
            shape(rows, width, BF16), shape(rest, width, BF16), shape(rows, 1, F32), shape(rest, 1, F32),
            shape(8, 128, F32), shape(rows, 1, F32),
        ),
        [HBM] * 2 + [VMEM] * 4, (VMEM,) * 9,
        [dma((rows // BLOCK,)), dma((rest // BLOCK,))], 4, product // 4, 16,
    )(image_emb, text_emb, cosine_multiplier.reshape(1, 1), logit_bias.reshape(1, 1), z1, inv1)
    near_block = lax.ppermute(zp, "dp", near)
    far2 = lax.ppermute(z2, "dp", far)
    coef, gq, along = call(
        local_kernel,
        (shape(rows, rows, BF16), shape(rows, width, F32), shape(rows, 1, F32)),
        [VMEM] * 3, (VMEM,) * 3, [], 8, 2 * product, 16,
    )(consts, zp, zq)
    grad = call(
        near_kernel, shape(rows, width, BF16),
        [VMEM] * 7, VMEM, [], 12, 3 * product,
    )(consts, zp, zq, coef, near_block, rawp, invp)
    so_far, along = call(
        far_kernel, (shape(rows, width, F32), shape(rows, 1, F32)),
        [VMEM] * 6, (VMEM,) * 2, [], 8, 2 * product * first // rows,
    )(consts, zq, far1, gq, along, grad)
    return call(
        last_kernel,
        (pltpu.HBM((rows, width), BF16),) * 2,
        [VMEM] * 11, (HBM, HBM),
        [pltpu.VMEM((rows, width), BF16), dma((rows // HALF,)), dma], 12, 2 * product * rest // rows,
    )(consts, zq, far2, so_far, along, ratio, raw1, raw2, inv1, inv2, grad)


def solution(mesh):
    in_specs = (P("dp", None), P("dp", None), P(), P())
    out_specs = (P("dp", None), P("dp", None))
    return jax.shard_map(
        on_device, mesh=mesh, in_specs=in_specs, out_specs=out_specs, check_vma=False
    )
```

```python
import functools

import jax
import jax.numpy as jnp
from jax import lax
from jax.experimental import pallas as pl
from jax.experimental.pallas import tpu as pltpu
from jax.sharding import PartitionSpec as P

epsilon = 1e-06
LOG2_E = 1.4426950408889634
F32, BF16 = jnp.float32, jnp.bfloat16
BLOCK = 256
HALF = BLOCK // 2
FIRST = 768
MIB = 2**20

VMEM = pl.BlockSpec(memory_space=pltpu.VMEM)
SMEM = pl.BlockSpec(memory_space=pltpu.SMEM)
HBM = pl.BlockSpec(memory_space=pl.ANY)


def rows_dot_rows(a, b):
    return lax.dot_general(a, b, (((1,), (1,)), ((), ())), preferred_element_type=F32)


def columns_dot(a, b):
    return lax.dot_general(a, b, (((0,), (0,)), ((), ())), preferred_element_type=F32)


def dot(a, b):
    return jnp.dot(a, b, preferred_element_type=F32)


def blocks(rows):
    return [slice(start, start + BLOCK) for start in range(0, rows, BLOCK)]


def fetch(parity, if_even, if_odd, start, target, sems):
    for i, here in enumerate(blocks(target.shape[0])):
        there = pl.ds(start + here.start, BLOCK)

        @pl.when(parity == 0)
        def _():
            pltpu.make_async_copy(if_even.at[there], target.at[here], sems.at[i]).start()

        @pl.when(parity == 1)
        def _():
            pltpu.make_async_copy(if_odd.at[there], target.at[here], sems.at[i]).start()


def arrived(source, target, sems, i, here):
    pltpu.make_async_copy(source.at[pl.ds(0, BLOCK)], target.at[here], sems.at[i]).wait()


def normalize_block(raw):
    floats = raw.astype(F32)
    inverse = lax.rsqrt(jnp.sum(floats * floats, axis=-1, keepdims=True) + epsilon)
    return (floats * inverse).astype(BF16), inverse


def my_parity():
    return lax.rem(lax.axis_index("dp"), 2)


def first_kernel(image, text, z1, raw1, inv1, sems):
    fetch(my_parity(), image, text, 0, raw1, sems)
    for i, here in enumerate(blocks(raw1.shape[0])):
        arrived(image, raw1, sems, i, here)
        z1[here, :], inv1[here, :] = normalize_block(raw1[here, :])


def rest_kernel(
    image, text, multiplier, bias, z1, zp, z2, zq, rawp, raw2, invp, inv2, consts, semsp, sems2
):
    first = z1.shape[0]
    parity = my_parity()
    fetch(parity, text, image, 0, rawp, semsp)
    fetch(parity, image, text, first, raw2, sems2)
    consts[0:1, :] = jnp.broadcast_to(multiplier[...], (1, consts.shape[1]))
    consts[1:2, :] = jnp.broadcast_to(bias[...], (1, consts.shape[1]))
    zq[:first, :] = z1[...]
    for i, here in enumerate(blocks(rawp.shape[0])):
        arrived(image, rawp, semsp, i, here)
        zp[here, :], invp[here, :] = normalize_block(rawp[here, :])
    for i, here in enumerate(blocks(raw2.shape[0])):
        arrived(image, raw2, sems2, i, here)
        normed, inv2[here, :] = normalize_block(raw2[here, :])
        z2[here, :] = normed
        zq[pl.ds(first + here.start, BLOCK), :] = normed


def constants(consts):
    multiplier, bias = consts[0:1, 0:1], consts[1:2, 0:1]
    return multiplier, -multiplier * LOG2_E, -bias * LOG2_E


def exponential(agreement, scale, shift):
    return jnp.exp2(agreement * scale + shift)


def local_kernel(consts, zp, zq, coef, gq):
    multiplier, scale, shift = constants(consts)
    count = zq.shape[0]
    for here in blocks(zp.shape[0]):
        power = exponential(rows_dot_rows(zp[here, :], zq[...]), scale, shift)
        value = multiplier / (1.0 + power)
        row = lax.broadcasted_iota(jnp.int32, (BLOCK, count), 0) + here.start
        column = lax.broadcasted_iota(jnp.int32, (BLOCK, count), 1)
        coef[here, :] = jnp.where(row == column, -power * value, value).astype(BF16)
    for here in blocks(count):
        gq[here, :] = columns_dot(coef[:, here], zp[...])


def backward(raw, inverse, upstream):
    floats = raw.astype(F32)
    inner = jnp.sum(floats * upstream, axis=-1, keepdims=True)
    return inverse * (upstream - floats * (inverse * inverse * inner))


def near_kernel(consts, zp, zq, coef, other, rawp, invp, grad):
    multiplier, scale, shift = constants(consts)
    for here in blocks(zp.shape[0]):
        total = dot(coef[here, :], zq[...])
        power = exponential(rows_dot_rows(zp[here, :], other[...]), scale, shift)
        factors = (multiplier / (1.0 + power)).astype(BF16)
        total = total + dot(factors, other[...])
        grad[here, :] = backward(rawp[here, :], invp[here, :], total).astype(BF16)


def put(parity, if_even, if_odd, there, source, sem):
    @pl.when(parity == 0)
    def _():
        pltpu.make_async_copy(source, if_even.at[there], sem).start()

    @pl.when(parity == 1)
    def _():
        pltpu.make_async_copy(source, if_odd.at[there], sem).start()


def raw_block(here, raw1, raw2, inv1, inv2):
    first = raw1.shape[0]
    if here.start < first:
        return raw1[here, :], inv1[here, :]
    there = slice(here.start - first, here.stop - first)
    return raw2[there, :], inv2[there, :]


def far_kernel(consts, zq, other, gq, after_near, so_far):
    multiplier, scale, shift = constants(consts)
    pieces = blocks(zq.shape[0])
    ahead = rows_dot_rows(zq[pieces[0], :], other[...])
    for i, here in enumerate(pieces):
        agreement = ahead
        if i + 1 < len(pieces):
            ahead = rows_dot_rows(zq[pieces[i + 1], :], other[...])
        factors = (multiplier / (1.0 + exponential(agreement, scale, shift))).astype(BF16)
        so_far[here, :] = gq[here, :] + dot(factors, other[...])


def last_kernel(
    consts, zq, other, so_far, raw1, raw2, inv1, inv2, grad, image_out, text_out, held, sems, grad_sem
):
    multiplier, scale, shift = constants(consts)
    parity = my_parity()
    everything = pl.ds(0, grad.shape[0])
    put(parity, text_out, image_out, everything, grad, grad_sem)
    pieces = blocks(zq.shape[0])
    ahead = rows_dot_rows(zq[pieces[0], :], other[...])
    for i, here in enumerate(pieces):
        agreement = ahead
        if i + 1 < len(pieces):
            ahead = rows_dot_rows(zq[pieces[i + 1], :], other[...])
        factors = (multiplier / (1.0 + exponential(agreement, scale, shift))).astype(BF16)
        total = so_far[here, :] + dot(factors, other[...])
        raw, inverse = raw_block(here, raw1, raw2, inv1, inv2)
        for j in range(2):
            half = slice(j * HALF, (j + 1) * HALF)
            there = slice(here.start + half.start, here.start + half.stop)
            held[there, :] = backward(raw[half, :], inverse[half, :], total[half, :]).astype(BF16)
            put(parity, image_out, text_out, there, held.at[there], sems.at[2 * i + j])
    pltpu.make_async_copy(grad, image_out.at[everything], grad_sem).wait()
    for i in range(zq.shape[0] // HALF):
        there = pl.ds(i * HALF, HALF)
        pltpu.make_async_copy(held.at[there], image_out.at[there], sems.at[i]).wait()


def shape(rows, columns, kind):
    return jax.ShapeDtypeStruct((rows, columns), kind)


def call(kernel, out_shape, in_specs, out_specs, scratch, limit, flops, weight=1, **more):
    return pl.pallas_call(
        kernel,
        out_shape=out_shape,
        in_specs=in_specs,
        out_specs=out_specs,
        scratch_shapes=scratch,
        compiler_params=pltpu.CompilerParams(vmem_limit_bytes=limit * MIB),
        cost_estimate=pl.CostEstimate(
            flops=flops * weight, bytes_accessed=flops, transcendentals=0
        ),
        **more,
    )


def on_device(image_emb, text_emb, cosine_multiplier, logit_bias):
    rows, width = image_emb.shape
    count = lax.axis_size("dp")
    near = [(e, e ^ 1) for e in range(count)]
    far = [(e, (e - 1) % count if e % 2 == 0 else (e + 1) % count) for e in range(count)]
    first, rest = FIRST, rows - FIRST
    image_emb = pltpu.with_memory_space_constraint(image_emb, pltpu.HBM)
    text_emb = pltpu.with_memory_space_constraint(text_emb, pltpu.HBM)
    dma = pltpu.SemaphoreType.DMA
    product = 2 * rows * rows * width

    z1, raw1, inv1 = call(
        first_kernel,
        (shape(first, width, BF16), shape(first, width, BF16), shape(first, 1, F32)),
        [HBM, HBM], (VMEM,) * 3, [dma((first // BLOCK,))], 4, product // 8, 16,
    )(image_emb, text_emb)
    far1 = lax.ppermute(z1, "dp", far)
    zp, z2, zq, rawp, raw2, invp, inv2, consts = call(
        rest_kernel,
        (
            shape(rows, width, BF16), shape(rest, width, BF16), shape(rows, width, BF16),
            shape(rows, width, BF16), shape(rest, width, BF16), shape(rows, 1, F32), shape(rest, 1, F32),
            shape(8, 128, F32),
        ),
        [HBM] * 2 + [VMEM] * 3, (VMEM,) * 8,
        [dma((rows // BLOCK,)), dma((rest // BLOCK,))], 4, product // 4, 16,
    )(image_emb, text_emb, cosine_multiplier.reshape(1, 1), logit_bias.reshape(1, 1), z1)
    near_block = lax.ppermute(zp, "dp", near)
    far2 = lax.ppermute(z2, "dp", far)
    coef, gq = call(
        local_kernel,
        (shape(rows, rows, BF16), shape(rows, width, F32)),
        [VMEM] * 3, (VMEM,) * 2, [], 8, 2 * product, 16,
    )(consts, zp, zq)
    grad = call(
        near_kernel, shape(rows, width, BF16),
        [VMEM] * 7, VMEM, [], 12, 3 * product,
    )(consts, zp, zq, coef, near_block, rawp, invp)
    so_far = call(
        far_kernel, shape(rows, width, F32),
        [VMEM] * 5, VMEM, [], 8, 2 * product * first // rows,
    )(consts, zq, far1, gq, grad)
    return call(
        last_kernel,
        (pltpu.HBM((rows, width), BF16),) * 2,
        [VMEM] * 9, (HBM, HBM),
        [pltpu.VMEM((rows, width), BF16), dma((rows // HALF,)), dma], 12, 2 * product * rest // rows,
    )(consts, zq, far2, so_far, raw1, raw2, inv1, inv2, grad)


def solution(mesh):
    in_specs = (P("dp", None), P("dp", None), P(), P())
    out_specs = (P("dp", None), P("dp", None))
    return jax.shard_map(
        on_device, mesh=mesh, in_specs=in_specs, out_specs=out_specs, check_vma=False
    )
```
